32 devices in a mesh: seq: 8 (over z, x), dp: 4 (over y, core).
Axes of the slice: x: 2, y: 2, z: 4, core: 2. Of those that a mesh axis runs over, the one named last changes fastest.
Arguments:
- layer_input: bfloat16 [16384, 576], P(('seq', 'dp')), may hold values from -6 to 6
- w_qkv: bfloat16 [552960], P(('seq', 'dp')), may hold values from -0.25 to 0.25
- w_out: bfloat16 [331776], P(('seq', 'dp')), may hold values from -4 to 4
- w_gu: bfloat16 [1769472], P(('seq', 'dp')), may hold values from -0.25 to 0.25
- w_down: bfloat16 [884736], P(('seq', 'dp')), may hold values from -0.15625 to 0.15625
- norm_gains: float32 [2, 576], replicated, may hold values from 0.1 to 1.9
- lengths: int32 [4, 6], P('dp'), may hold values from 1 to 2048, 4096 in all within a row
- cotangent: bfloat16 [16384, 576], P(('seq', 'dp')), may hold values from -6 to 6
Outputs:
- layer_output: bfloat16 [16384, 576], P(('seq', 'dp'))
- input_grad: float32 [16384, 576], P(('seq', 'dp'))
- g_qkv: float32 [552960], P(('seq', 'dp'))
- g_out: float32 [331776], P(('seq', 'dp'))
- g_gu: float32 [1769472], P(('seq', 'dp'))
- g_down: float32 [884736], P(('seq', 'dp'))
- gains_grad: float32 [2, 576], replicated
The draws below stay inside these ranges and needn't reach their ends.
Inputs may be any that keep to these rules, and one draw needn't show every extreme that they name: Each row lists the lengths of the 6 sequences of one dp group in order; a row sums to 4096, and its largest entry is exactly 2048.
All inputs are finite; a program needn't handle non-finite values.
Results may differ from the reference program's by a relative error of at most 0.012.
Values may be sent and summed in bfloat16 or wider, within the bound.
A program may use at most 128 MiB of HBM per device.

```python
import math
import jax
import jax.numpy as jnp
import numpy as np
from jax import lax

D = 576
QUERY_HEADS = 9
KEY_VALUE_HEADS = 3
HEAD_SIZE = 64
FF = 1536
TOK_DEV = 512
NDOCS = 6
GROUP = 4096
MAXLEN = 2048
QKV = 960
TOKENS = 16384
N_SEQ = 8
N_DP = 4


def block_scale(rng, dims, shards, least, top_value):
    def one(position, shards_of):
        steps = jax.random.uniform(jax.random.fold_in(jax.random.fold_in(rng, 6), position), (shards_of,), jnp.float32, least / len(shards), top_value / len(shards))
        return jnp.repeat(jnp.exp(steps), dims[position] // shards_of).reshape((-1,) + (1,) * (len(dims) - position - 1))

    factor_of = one(*shards[0])
    for cut in shards[1:]:
        factor_of = factor_of * one(*cut)
    return factor_of


def profile(number_of, total, limit, skew):
    weights = [(1 << 20) // math.isqrt(grade ** skew) + 1 for grade in range(2, number_of + 1)]
    spare, holding = total - limit - (number_of - 1), [1] * (number_of - 1)
    while spare > 0:
        free = [i for i in range(number_of - 1) if holding[i] < limit]
        mass, left = sum([weights[i] for i in free]), spare
        for i in free:
            addition = min(limit - holding[i], max(1, left * weights[i] // mass), spare)
            holding[i] = holding[i] + addition
            spare = spare - addition
    return np.array([limit] + holding)


def ragged(own_key, amount, total, reach, lean):
    if amount == 2:
        one = jax.random.randint(own_key, (), max(1, total - reach), min(reach, total - 1) + 1)
        return jnp.stack([one, total - one])
    tallies = jnp.asarray(profile(amount, total, reach, lean), jnp.int32)
    pairs = (amount - 1) // 2
    donor, sink = tallies[1:1 + 2 * pairs:2], tallies[2:2 + 2 * pairs:2]
    slack = jnp.minimum(donor - 1, reach - sink)
    passed = jax.random.randint(jax.random.fold_in(own_key, 1), (pairs,), 0, 1 << 20) % (slack + 1)
    tallies = tallies.at[1:1 + 2 * pairs:2].set(donor - passed).at[2:2 + 2 * pairs:2].set(sink + passed)
    return tallies[jax.random.permutation(jax.random.fold_in(own_key, 2), amount)]


def normal_values(own_key, shape, scale, reach, shards=(), held_as=jnp.bfloat16):
    values = scale * jax.random.normal(own_key, shape, jnp.float32)
    if shards:
        values = values * block_scale(own_key, shape, shards, -0.22, 0.18)
    return jnp.clip(values, -reach, reach).astype(held_as)


def setup_inputs(seed: int = 0) -> dict:
    splits = jax.random.split(jax.random.key(seed), 9)
    layer_input = normal_values(splits[0], (TOKENS, D), 1.0, 6.0, ((0, 32),))
    w_qkv = normal_values(splits[1], (D * QKV,), D ** -0.5, 0.25, ((0, 32),))
    w_out = normal_values(splits[2], (QUERY_HEADS * HEAD_SIZE * D,), 2 ** -0.5, 4.0, ((0, 32),))
    w_gu = normal_values(splits[3], (2 * D * FF,), D ** -0.5, 0.25, ((0, 32),))
    w_down = normal_values(splits[4], (FF * D,), FF ** -0.5, 0.15625, ((0, 32),))
    norm_gains = jnp.clip(1.0 + 0.18 * jax.random.normal(splits[5], (2, D), jnp.float32), 0.1, 1.9)
    lengths = jax.vmap(lambda own: ragged(own, NDOCS, GROUP, MAXLEN, 2))(jax.random.split(splits[6], N_DP)).reshape((N_DP, NDOCS)).astype(jnp.int32)
    cotangent = normal_values(splits[7], (TOKENS, D), 1.0, 6.0, ((0, 32),))
    return {"layer_input": layer_input, "w_qkv": w_qkv, "w_out": w_out, "w_gu": w_gu, "w_down": w_down, "norm_gains": norm_gains, "lengths": lengths, "cotangent": cotangent}


@jax.custom_vjp
def lower_precision(v):
    return lax.optimization_barrier(v.astype(jnp.bfloat16)).astype(jnp.float32)

@jax.custom_vjp
def lower_precision_back(v):
    return v

def low_keep(v):
    return (lower_precision(v), None)

def low_pass(kept, grad):
    return (grad,)

def back_keep(v):
    return (v, None)

def back_low(kept, grad):
    return (lower_precision(grad),)
lower_precision.defvjp(low_keep, low_pass)
lower_precision_back.defvjp(back_keep, back_low)
EPS = 1e-05
THETA = 100000.0
MASKED = -1e+30
HIGH = lax.Precision.HIGHEST

def rms_norm(value_rows, gain):
    return value_rows * lax.rsqrt(lax.optimization_barrier(jnp.mean(value_rows * value_rows, axis=-1, keepdims=True)) + EPS) * gain

def apply_rotary(value_rows, token_position):
    half = value_rows.shape[-1] // 2
    freq = jnp.exp(jnp.arange(half, dtype=jnp.float32) * (-2.0 * math.log(THETA) / value_rows.shape[-1]))
    angle = token_position.astype(jnp.float32)[:, None] * freq[None, :]
    cosine = jnp.cos(angle)[:, None, :]
    sine = jnp.sin(angle)[:, None, :]
    first = value_rows[..., :half]
    second = value_rows[..., half:]
    return jnp.concatenate([first * cosine - second * sine, second * cosine + first * sine], axis=-1)

def layout(lengths_row, index):
    ends = jnp.cumsum(lengths_row, dtype=jnp.int32)
    done = ends[None, :] <= index[:, None]
    segment_index = lax.optimization_barrier(jnp.sum(done.astype(jnp.int32), axis=1, dtype=jnp.int32))
    token_position = index - lax.optimization_barrier(jnp.sum(jnp.where(done, lengths_row[None, :], 0), axis=1, dtype=jnp.int32))
    return (segment_index, token_position)

def group_attention(query_rows, key_rows, value_rows, segment_index):
    count_total = query_rows.shape[0]
    row_count = min(512, count_total)
    scale = 1.0 / math.sqrt(HEAD_SIZE)
    index = jnp.arange(count_total, dtype=jnp.int32)
    grouped_heads = query_rows.reshape(count_total // row_count, row_count, KEY_VALUE_HEADS, QUERY_HEADS // KEY_VALUE_HEADS, HEAD_SIZE)

    def one_block(args):
        block_query, block_segment, block_index = args
        scores = lower_precision_back(jnp.einsum('tkgd,skd->kgts', block_query, key_rows, precision=HIGH) * scale)
        allowed = (block_segment[:, None] == segment_index[None, :]) & (block_index[:, None] >= index[None, :])
        scores = jnp.where(allowed[None, None], scores, MASKED)
        weights = lower_precision(jax.nn.softmax(scores, axis=-1))
        return jnp.einsum('kgts,skd->tkgd', weights, value_rows, precision=HIGH)
    result = lax.map(jax.checkpoint(one_block), (grouped_heads, segment_index.reshape(-1, row_count), index.reshape(-1, row_count)))
    return result.reshape(count_total, QUERY_HEADS * HEAD_SIZE)

def forward(inputs, mixing_in, mixing_out, expand_matrix, shrink_matrix, gains, segment_index, token_position):
    token_count = inputs.shape[0]
    query_width = QUERY_HEADS * HEAD_SIZE
    key_width = KEY_VALUE_HEADS * HEAD_SIZE
    normed = lower_precision(rms_norm(inputs, gains[0]))
    projected_output = jnp.dot(normed, mixing_in, precision=HIGH)
    query_rows = lower_precision(apply_rotary(lower_precision_back(projected_output[:, :query_width]).reshape(token_count, QUERY_HEADS, HEAD_SIZE), token_position))
    key_rows = lower_precision(apply_rotary(lower_precision_back(projected_output[:, query_width:query_width + key_width]).reshape(token_count, KEY_VALUE_HEADS, HEAD_SIZE), token_position))
    value_rows = lower_precision(lower_precision_back(projected_output[:, query_width + key_width:])).reshape(token_count, KEY_VALUE_HEADS, HEAD_SIZE)

    def query_per_group(args):
        return group_attention(args[0], args[1], args[2], args[3])
    attended_rows = lax.map(query_per_group, (query_rows.reshape(N_DP, -1, QUERY_HEADS, HEAD_SIZE), key_rows.reshape(N_DP, -1, KEY_VALUE_HEADS, HEAD_SIZE), value_rows.reshape(N_DP, -1, KEY_VALUE_HEADS, HEAD_SIZE), segment_index))
    attended_rows = lower_precision(lower_precision_back(attended_rows.reshape(token_count, query_width)))
    mid = inputs + lower_precision_back(jnp.dot(attended_rows, mixing_out, precision=HIGH))
    normed_two = lower_precision(rms_norm(mid, gains[1]))
    gate_up = lower_precision_back(jnp.dot(normed_two, expand_matrix, precision=HIGH))
    hidden = lower_precision(jax.nn.silu(gate_up[:, :FF]) * gate_up[:, FF:])
    return mid + jnp.dot(hidden, shrink_matrix, precision=HIGH)

def reference(layer_input, w_qkv, w_out, w_gu, w_down, norm_gains, lengths, cotangent):
    group = N_SEQ * TOK_DEV

    def to_groups(array):
        return array.reshape(N_SEQ, N_DP, TOK_DEV, D).transpose(1, 0, 2, 3).reshape(N_DP * group, D)

    def from_groups(array):
        return array.reshape(N_DP, N_SEQ, TOK_DEV, D).transpose(1, 0, 2, 3).reshape(N_DP * group, D)
    index = jnp.arange(group, dtype=jnp.int32)
    segment_index, token_position = jax.vmap(lambda row: layout(row, index))(lengths)
    flat_position = token_position.reshape(-1)
    inputs = to_groups(layer_input.astype(jnp.float32))
    grad_out = to_groups(cotangent.astype(jnp.float32))
    mixing_in = w_qkv.astype(jnp.float32).reshape(D, -1)
    mixing_out = w_out.astype(jnp.float32).reshape(QUERY_HEADS * HEAD_SIZE, D)
    expand_matrix = w_gu.astype(jnp.float32).reshape(D, 2 * FF)
    shrink_matrix = w_down.astype(jnp.float32).reshape(FF, D)

    def run(inputs, mixing_in, mixing_out, expand_matrix, shrink_matrix, gains):
        return forward(inputs, mixing_in, mixing_out, expand_matrix, shrink_matrix, gains, segment_index, flat_position)
    result, pullback = jax.vjp(run, inputs, mixing_in, mixing_out, expand_matrix, shrink_matrix, norm_gains.astype(jnp.float32))
    grads = pullback(grad_out)
    return (from_groups(result).astype(jnp.bfloat16), from_groups(grads[0]), grads[1].reshape(-1), grads[2].reshape(-1), grads[3].reshape(-1), grads[4].reshape(-1), grads[5])
```

```python
import math

import jax
import jax.numpy as jnp
from jax import lax
from jax.sharding import PartitionSpec as P

D = 576
QUERY_HEADS = 9
KEY_VALUE_HEADS = 3
HEAD_SIZE = 64
FF = 1536


EPS = 1e-05
THETA = 100000.0
MASKED = -1e30


def rms_norm(value_rows, gain):
    return (
        value_rows
        * lax.rsqrt(jnp.mean(value_rows * value_rows, axis=-1, keepdims=True) + EPS)
        * gain
    )


def apply_rotary(value_rows, token_position):
    half = value_rows.shape[-1] // 2
    freq = jnp.exp(
        jnp.arange(half, dtype=jnp.float32) * (-2.0 * math.log(THETA) / value_rows.shape[-1])
    )
    angle = token_position.astype(jnp.float32)[:, None] * freq[None, :]
    cosine = jnp.cos(angle)[:, None, :]
    sine = jnp.sin(angle)[:, None, :]
    first = value_rows[..., :half]
    second = value_rows[..., half:]
    return jnp.concatenate(
        [first * cosine - second * sine, second * cosine + first * sine], axis=-1
    )


def layout(lengths_row, index):
    count = lengths_row.shape[0]
    earlier = jnp.arange(count)[:, None] >= jnp.arange(count)[None, :]
    ends = jnp.sum(jnp.where(earlier, lengths_row[None, :], 0), axis=1, dtype=jnp.int32)
    done = ends[None, :] <= index[:, None]
    segment_index = jnp.sum(done.astype(jnp.int32), axis=1, dtype=jnp.int32)
    token_position = index - jnp.sum(
        jnp.where(done, lengths_row[None, :], 0), axis=1, dtype=jnp.int32
    )
    return (segment_index, token_position)


def silu_product(gate_up):
    width = gate_up.shape[1] // 2
    return jax.nn.silu(gate_up[:, :width]) * gate_up[:, width:]


def per_device(layer_input, w_qkv, w_out, w_gu, w_down, norm_gains, lengths, cotangent):
    token_rows = layer_input.shape[0]
    seq_count = lax.axis_size("seq")
    group = token_rows * seq_count
    heads_per_group = QUERY_HEADS // KEY_VALUE_HEADS
    query_width = QUERY_HEADS * HEAD_SIZE
    key_width = KEY_VALUE_HEADS * HEAD_SIZE
    scale = 1.0 / math.sqrt(HEAD_SIZE)
    block_current = math.gcd(group, 512)
    blocks = group // block_current
    numbers = jnp.arange(blocks, dtype=jnp.int32)

    def fetch_weights():
        parts = (
            lax.all_gather(w_qkv, ("seq", "dp"), axis=0, tiled=True),
            lax.all_gather(w_out, ("seq", "dp"), axis=0, tiled=True),
            lax.all_gather(w_gu, ("seq", "dp"), axis=0, tiled=True),
            lax.all_gather(w_down, ("seq", "dp"), axis=0, tiled=True),
        )
        return (
            parts[0].reshape(D, -1),
            parts[1].reshape(query_width, D),
            parts[2].reshape(D, 2 * FF),
            parts[3].reshape(FF, D),
        )

    def fetch_pairs(keys_mine, values_mine):
        return (
            lax.all_gather(keys_mine, "seq", axis=0, tiled=True),
            lax.all_gather(values_mine, "seq", axis=0, tiled=True),
        )

    lengths_row = lengths[0]
    query_index = lax.axis_index("seq") * token_rows + jnp.arange(token_rows, dtype=jnp.int32)
    query_segment, query_token_position = layout(lengths_row, query_index)
    key_index = jnp.arange(group, dtype=jnp.int32)
    key_valid = key_index >= 0
    key_segment = layout(lengths_row, jnp.maximum(key_index, 0))[0]

    def block_parts(key_value_pairs, number):
        start_offset = number * block_current
        key_window_part = lax.dynamic_slice_in_dim(
            key_value_pairs[0], start_offset, block_current, 0
        ).reshape(block_current, KEY_VALUE_HEADS, HEAD_SIZE)
        value_window_part = lax.dynamic_slice_in_dim(
            key_value_pairs[1], start_offset, block_current, 0
        ).reshape(block_current, KEY_VALUE_HEADS, HEAD_SIZE)
        seg_slice = lax.dynamic_slice_in_dim(key_segment, start_offset, block_current, 0)
        idx_slice = lax.dynamic_slice_in_dim(key_index, start_offset, block_current, 0)
        valid_slice = lax.dynamic_slice_in_dim(key_valid, start_offset, block_current, 0)
        allowed = (
            valid_slice[None, :]
            & (query_segment[:, None] == seg_slice[None, :])
            & (query_index[:, None] >= idx_slice[None, :])
        )
        return (key_window_part, value_window_part, allowed[None, None])

    mixing_in, mixing_out, expand_matrix, shrink_matrix = fetch_weights()
    inputs = layer_input.astype(jnp.float32)
    normed, norm_back = jax.vjp(rms_norm, inputs, norm_gains[0])
    normed_low = normed.astype(jnp.bfloat16)
    projected_output = jnp.dot(normed_low, mixing_in, preferred_element_type=jnp.float32)
    rotated_query, query_unrot = jax.vjp(
        lambda part: apply_rotary(
            part.reshape(token_rows, QUERY_HEADS, HEAD_SIZE), query_token_position
        ),
        projected_output[:, :query_width],
    )
    keys_rot, unrotated_keys = jax.vjp(
        lambda part: apply_rotary(
            part.reshape(token_rows, KEY_VALUE_HEADS, HEAD_SIZE), query_token_position
        ),
        projected_output[:, query_width : query_width + key_width],
    )
    query_lower_precision = rotated_query.astype(jnp.bfloat16).reshape(
        token_rows, KEY_VALUE_HEADS, heads_per_group, HEAD_SIZE
    )
    keys_low = keys_rot.astype(jnp.bfloat16).reshape(token_rows, key_width)
    values_low = projected_output[:, query_width + key_width :].astype(jnp.bfloat16)
    pairs_now = fetch_pairs(keys_low, values_low)

    def scores_of(key_window_part, allowed):
        raw = (
            jnp.einsum(
                "tkgd,skd->kgts",
                query_lower_precision,
                key_window_part,
                preferred_element_type=jnp.float32,
            )
            * scale
        )
        return jnp.where(allowed, raw, MASKED)

    statistic_dims = (KEY_VALUE_HEADS, heads_per_group, token_rows)

    def stat_step(carry, number):
        key_window_part, value_window_part, allowed = block_parts(pairs_now, number)
        scores = scores_of(key_window_part, allowed)
        highest = jnp.maximum(carry[0], jnp.max(scores, axis=-1))
        summed = carry[1] * jnp.exp(carry[0] - highest) + jnp.sum(
            jnp.where(allowed, jnp.exp(scores - highest[..., None]), 0.0), axis=-1
        )
        return ((highest, summed), None)

    stats = lax.scan(
        stat_step,
        (jnp.full(statistic_dims, MASKED, jnp.float32), jnp.zeros(statistic_dims, jnp.float32)),
        numbers,
    )[0]
    log_total = stats[0] + jnp.log(stats[1])

    def probs_of(key_value_pairs, number):
        key_window_part, value_window_part, allowed = block_parts(key_value_pairs, number)
        scores = scores_of(key_window_part, allowed)
        probs = jnp.where(allowed, jnp.exp(scores - log_total[..., None]), 0.0)
        return (key_window_part, value_window_part, probs)

    def out_step(summed, number):
        key_window_part, value_window_part, probs = probs_of(pairs_now, number)
        return (
            summed
            + jnp.einsum(
                "kgts,skd->tkgd",
                probs.astype(jnp.bfloat16),
                value_window_part,
                preferred_element_type=jnp.float32,
            ),
            None,
        )

    head_layout_dims = (token_rows, KEY_VALUE_HEADS, heads_per_group, HEAD_SIZE)
    attended_rows = lax.scan(out_step, jnp.zeros(head_layout_dims, jnp.float32), numbers)[0]
    attended_low = attended_rows.reshape(token_rows, query_width).astype(jnp.bfloat16)
    mid = inputs + jnp.dot(attended_low, mixing_out, preferred_element_type=jnp.float32)
    normed_two, norm_two_back = jax.vjp(rms_norm, mid, norm_gains[1])
    normed_two_low = normed_two.astype(jnp.bfloat16)
    gate_up = jnp.dot(normed_two_low, expand_matrix, preferred_element_type=jnp.float32)
    hidden, hidden_back = jax.vjp(silu_product, gate_up)
    hidden_low = hidden.astype(jnp.bfloat16)
    result = (mid + jnp.dot(hidden_low, shrink_matrix, preferred_element_type=jnp.float32)).astype(
        jnp.bfloat16
    )
    mixing_in, mixing_out, expand_matrix, shrink_matrix = fetch_weights()
    pairs_back = fetch_pairs(keys_low, values_low)
    grad_down = jnp.einsum("tf,td->fd", hidden_low, cotangent, preferred_element_type=jnp.float32)
    d_hidden = jnp.einsum("td,fd->tf", cotangent, shrink_matrix, preferred_element_type=jnp.float32)
    d_gate_up = hidden_back(d_hidden)[0].astype(jnp.bfloat16)
    grad_expand = jnp.einsum(
        "td,tf->df", normed_two_low, d_gate_up, preferred_element_type=jnp.float32
    )
    d_normed_two = jnp.einsum(
        "tf,df->td", d_gate_up, expand_matrix, preferred_element_type=jnp.float32
    )
    d_mid_part, grad_gain_two = norm_two_back(d_normed_two)
    d_mid = cotangent.astype(jnp.float32) + d_mid_part
    d_branch = d_mid.astype(jnp.bfloat16)
    grad_mixing_out = jnp.einsum(
        "tq,td->qd", attended_low, d_branch, preferred_element_type=jnp.float32
    )
    d_attended = (
        jnp.einsum("td,qd->tq", d_branch, mixing_out, preferred_element_type=jnp.float32)
        .astype(jnp.bfloat16)
        .reshape(head_layout_dims)
    )
    delta = jnp.sum(d_attended.astype(jnp.float32) * attended_rows, axis=-1).transpose(1, 2, 0)

    def grad_step(d_query, number):
        key_window_part, value_window_part, probs = probs_of(pairs_back, number)
        d_probs = jnp.einsum(
            "tkgd,skd->kgts", d_attended, value_window_part, preferred_element_type=jnp.float32
        )
        d_scores = (probs * (d_probs - delta[..., None])).astype(jnp.bfloat16)
        new_query = (
            d_query
            + jnp.einsum(
                "kgts,skd->tkgd", d_scores, key_window_part, preferred_element_type=jnp.float32
            )
            * scale
        )
        d_keys = (
            jnp.einsum(
                "kgts,tkgd->skd",
                d_scores,
                query_lower_precision,
                preferred_element_type=jnp.float32,
            )
            * scale
        )
        d_values = jnp.einsum(
            "kgts,tkgd->skd",
            probs.astype(jnp.bfloat16),
            d_attended,
            preferred_element_type=jnp.float32,
        )
        return (
            new_query,
            (d_keys.reshape(block_current, key_width), d_values.reshape(block_current, key_width)),
        )

    d_query, key_value_rows = lax.scan(grad_step, jnp.zeros(head_layout_dims, jnp.float32), numbers)
    local_key_gradient = lax.psum_scatter(
        key_value_rows[0].reshape(group, key_width).astype(jnp.bfloat16),
        "seq",
        scatter_dimension=0,
        tiled=True,
    ).astype(jnp.float32)
    d_values_mine = lax.psum_scatter(
        key_value_rows[1].reshape(group, key_width).astype(jnp.bfloat16),
        "seq",
        scatter_dimension=0,
        tiled=True,
    ).astype(jnp.float32)
    d_query_pre = query_unrot(d_query.reshape(token_rows, QUERY_HEADS, HEAD_SIZE))[0]
    prior_key_gradient = unrotated_keys(
        local_key_gradient.reshape(token_rows, KEY_VALUE_HEADS, HEAD_SIZE)
    )[0]
    d_projected = jnp.concatenate([d_query_pre, prior_key_gradient, d_values_mine], axis=1).astype(
        jnp.bfloat16
    )
    grad_mixing_in = jnp.einsum(
        "td,tq->dq", normed_low, d_projected, preferred_element_type=jnp.float32
    )
    d_normed = jnp.einsum("tq,dq->td", d_projected, mixing_in, preferred_element_type=jnp.float32)
    d_input_part, grad_gain_one = norm_back(d_normed)
    d_input = d_mid + d_input_part
    summed_grads = (
        lax.psum_scatter(
            grad_mixing_in.reshape(-1), ("seq", "dp"), scatter_dimension=0, tiled=True
        ),
        lax.psum_scatter(
            grad_mixing_out.reshape(-1), ("seq", "dp"), scatter_dimension=0, tiled=True
        ),
        lax.psum_scatter(grad_expand.reshape(-1), ("seq", "dp"), scatter_dimension=0, tiled=True),
        lax.psum_scatter(grad_down.reshape(-1), ("seq", "dp"), scatter_dimension=0, tiled=True),
    )
    gain_grads = lax.psum(jnp.stack([grad_gain_one, grad_gain_two]), ("seq", "dp"))
    return (
        result,
        d_input,
        summed_grads[0],
        summed_grads[1],
        summed_grads[2],
        summed_grads[3],
        gain_grads,
    )


def solution(mesh):
    return jax.shard_map(
        per_device,
        mesh=mesh,
        in_specs=(
            P(("seq", "dp"), None),
            P(("seq", "dp")),
            P(("seq", "dp")),
            P(("seq", "dp")),
            P(("seq", "dp")),
            P(),
            P("dp", None),
            P(("seq", "dp"), None),
        ),
        out_specs=(
            P(("seq", "dp"), None),
            P(("seq", "dp"), None),
            P(("seq", "dp")),
            P(("seq", "dp")),
            P(("seq", "dp")),
            P(("seq", "dp")),
            P(),
        ),
        check_vma=False,
    )
```

```python
import functools
import math

import jax
import jax.numpy as jnp
from jax import lax
from jax.experimental import pallas as pl
from jax.experimental.pallas import tpu as pltpu
from jax.sharding import PartitionSpec as P

D = 576
QUERY_HEADS = 9
KEY_VALUE_HEADS = 3
HEAD_SIZE = 64
FF = 1536
HG = QUERY_HEADS // KEY_VALUE_HEADS

EPS = 1e-05
THETA = 100000.0
MASKED = -1e30
MESH = pl.DeviceIdType.MESH
BLK = 256
VMEM_LIMIT = 56 * 1024 * 1024
ORDERS = ((0, 2, 1), (1, 0, 2))


def rms_norm(value_rows, gain):
    return (
        value_rows
        * lax.rsqrt(jnp.mean(value_rows * value_rows, axis=-1, keepdims=True) + EPS)
        * gain
    )


def layout(lengths_row, index):
    count = lengths_row.shape[0]
    earlier = jnp.arange(count)[:, None] >= jnp.arange(count)[None, :]
    ends = jnp.sum(jnp.where(earlier, lengths_row[None, :], 0), axis=1, dtype=jnp.int32)
    done = ends[None, :] <= index[:, None]
    return jnp.sum(jnp.where(done, lengths_row[None, :], 0), axis=1, dtype=jnp.int32)


def silu_product(gate_up):
    width = gate_up.shape[1] // 2
    return jax.nn.silu(gate_up[:, :width]) * gate_up[:, width:]


def grid_sizes(seq_count, dp_count):
    return (seq_count // 2, 2, dp_count // 2, 2)


def coords():
    seq, dp = lax.axis_index("seq"), lax.axis_index("dp")
    return [seq // 2, seq % 2, dp // 2, dp % 2]


def device_at(coord):
    return (coord[0] * 2 + coord[1], coord[2] * 2 + coord[3])


def moved(me, sizes, axis, step):
    other = list(me)
    other[axis] = lax.rem(me[axis] + step + sizes[axis], sizes[axis])
    return other


def greet(me, sizes):
    barrier = pltpu.get_barrier_semaphore()
    count = 0
    for axis in range(4):
        for step in range(1, sizes[axis]):
            pl.semaphore_signal(
                barrier,
                inc=1,
                device_id=device_at(moved(me, sizes, axis, step)),
                device_id_type=MESH,
            )
            count += 1
    pl.semaphore_wait(barrier, count)


def gather_kernel(sizes, parts, *refs):
    shards, outs = refs[:parts], refs[parts : 2 * parts]
    send, recv, core_send, core_recv, local = refs[2 * parts :]
    me = coords()
    greet(me, sizes)
    started = []
    for part in range(parts):
        own = pltpu.make_async_copy(
            shards[part], outs[part].at[me[0], me[1], me[2], me[3]], local.at[part]
        )
        own.start()
        started.append(own)
    for own in started:
        own.wait()

    def region(part, held, where):
        return outs[part].at[
            tuple(slice(None) if a in held else where[a] for a in range(3)) + (where[3],)
        ]

    def copy(part, phase, axis, held, step, arriving=False):
        where = moved(me, sizes, axis, -step) if arriving else me
        block = region(part, held, where)
        return pltpu.make_async_remote_copy(
            src_ref=block,
            dst_ref=block,
            send_sem=send.at[part, phase, step],
            recv_sem=recv.at[part, phase, step],
            device_id=device_at(moved(me, sizes, axis, step)),
            device_id_type=MESH,
        )

    def to_core(part, slot, held, where, arriving=False):
        there = moved(where, sizes, 3, 1) if arriving else where
        block = region(part, held, there)
        return pltpu.make_async_remote_copy(
            src_ref=block,
            dst_ref=block,
            send_sem=core_send.at[part, slot],
            recv_sem=core_recv.at[part, slot],
            device_id=device_at(moved(me, sizes, 3, 1)),
            device_id_type=MESH,
        )

    for part in range(parts):
        axis = ORDERS[part][0]
        for step in range(1, sizes[axis]):
            copy(part, 0, axis, (), step).start()
    pending = []
    for phase in range(3):
        for part in range(parts):
            axis = ORDERS[part][phase]
            held = ORDERS[part][:phase]
            for step in range(1, sizes[axis]):
                copy(part, phase, axis, held, step, arriving=True).wait_recv()
                if phase == 2:
                    origin = moved(me, sizes, axis, -step)
                    to_core(part, step, held, origin).start()
                    pending.append((part, step, held, origin))
            if phase < 2:
                following = ORDERS[part][phase + 1]
                for step in range(1, sizes[following]):
                    copy(part, phase + 1, following, ORDERS[part][: phase + 1], step).start()
            if phase == 1:
                to_core(part, 0, ORDERS[part][:2], me).start()
                pending.append((part, 0, ORDERS[part][:2], me))
    for part in range(parts):
        for phase in range(3):
            axis = ORDERS[part][phase]
            for step in range(1, sizes[axis]):
                copy(part, phase, axis, ORDERS[part][:phase], step).wait_send()
    for part, slot, held, origin in pending:
        to_core(part, slot, held, origin).wait_send()
        to_core(part, slot, held, origin, arriving=True).wait_recv()


def all_gather(shards, sizes, ident):
    parts = len(shards)
    most = max(sizes)
    return pl.pallas_call(
        functools.partial(gather_kernel, sizes, parts),
        out_shape=[jax.ShapeDtypeStruct(sizes + s.shape, s.dtype) for s in shards],
        in_specs=[pl.BlockSpec(memory_space=pltpu.VMEM)] * parts,
        out_specs=[pl.BlockSpec(memory_space=pltpu.VMEM)] * parts,
        scratch_shapes=[
            pltpu.SemaphoreType.DMA((parts, 3, most)),
            pltpu.SemaphoreType.DMA((parts, 3, most)),
            pltpu.SemaphoreType.DMA((parts, most)),
            pltpu.SemaphoreType.DMA((parts, most)),
            pltpu.SemaphoreType.DMA((parts,)),
        ],
        compiler_params=pltpu.CompilerParams(
            collective_id=ident, has_side_effects=True, vmem_limit_bytes=VMEM_LIMIT
        ),
        cost_estimate=pl.CostEstimate(flops=0, bytes_accessed=60_000_000, transcendentals=0),
    )(*shards)


def scatter_order(part):
    return (3,) + tuple(reversed(ORDERS[part]))


def scatter_kernel(sizes, parts, with_gains, *refs):
    n_in = parts + with_gains
    grads, outs = refs[:n_in], refs[n_in : 2 * n_in]
    rest = list(refs[2 * n_in :])
    arrived = [[rest.pop(0) for _ in range(4)] for _ in range(parts)]
    totals = [[rest.pop(0) for _ in range(3)] for _ in range(parts)]
    if with_gains:
        gain_arrived, gain_total = rest.pop(0), rest.pop(0)
        gain_send, gain_recv = rest.pop(0), rest.pop(0)
    send, recv = rest
    me = coords()
    greet(me, sizes)

    def held_ref(part, phase):
        return grads[part] if phase == 0 else totals[part][phase - 1]

    def view(part, phase, index):
        order = scatter_order(part)
        left = sorted(set(range(4)) - set(order[:phase]))
        return tuple(index if a == order[phase] else slice(None) for a in left)

    def copy(part, phase, step):
        axis = scatter_order(part)[phase]
        target = moved(me, sizes, axis, step)
        return pltpu.make_async_remote_copy(
            src_ref=held_ref(part, phase).at[view(part, phase, target[axis])],
            dst_ref=arrived[part][phase].at[step - 1],
            send_sem=send.at[part, phase, step],
            recv_sem=recv.at[part, phase, step],
            device_id=device_at(target),
            device_id_type=MESH,
        )

    def add(part, phase):
        axis = scatter_order(part)[phase]
        mine = held_ref(part, phase).at[view(part, phase, me[axis])]
        lead = mine.shape[:-2]
        others = arrived[part][phase]

        def total_at(place):
            value = mine[place].astype(jnp.float32)
            for step in range(1, sizes[axis]):
                value = value + others[(step - 1,) + place].astype(jnp.float32)
            return value

        if phase == 3:
            outs[part][...] = total_at((slice(None), slice(None)))
            return
        target = totals[part][phase]

        def body(flat, carry):
            place = []
            for size in reversed(lead):
                place.insert(0, lax.rem(flat, size))
                flat = flat // size
            place = tuple(place) + (slice(None), slice(None))
            target[place] = total_at(place).astype(target.dtype)
            return carry

        lax.fori_loop(0, math.prod(lead), body, 0)

    def gain_copy(phase, step):
        return pltpu.make_async_remote_copy(
            src_ref=gain_total.at[phase],
            dst_ref=gain_arrived.at[phase, step - 1],
            send_sem=gain_send.at[phase, step],
            recv_sem=gain_recv.at[phase, step],
            device_id=device_at(moved(me, sizes, phase, step)),
            device_id_type=MESH,
        )

    def start(phase, part):
        for step in range(1, sizes[scatter_order(part)[phase]]):
            copy(part, phase, step).start()

    def gain_start(phase):
        for step in range(1, sizes[phase]):
            gain_copy(phase, step).start()

    for part in range(parts):
        start(0, part)
    if with_gains:
        gain_total[0] = grads[parts][...]
        gain_start(0)
    for phase in range(4):
        for part in reversed(range(parts)):
            for step in range(1, sizes[scatter_order(part)[phase]]):
                copy(part, phase, step).wait_recv()
            add(part, phase)
            if phase < 3:
                start(phase + 1, part)
        if with_gains:
            value = gain_total[phase]
            for step in range(1, sizes[phase]):
                gain_copy(phase, step).wait_recv()
            slots = [value] + [gain_arrived[phase, s - 1] for s in range(1, sizes[phase])]
            value = sum(slots[1:], slots[0])
            if phase < 3:
                gain_total[phase + 1] = value
                gain_start(phase + 1)
            else:
                outs[parts][...] = value
    for phase in range(4):
        for part in range(parts):
            for step in range(1, sizes[scatter_order(part)[phase]]):
                copy(part, phase, step).wait_send()
        if with_gains:
            for step in range(1, sizes[phase]):
                gain_copy(phase, step).wait_send()


def reduce_scatter(grads, gains, sizes, ident):
    parts = len(grads)
    most = max(sizes)
    scratch = []
    for part in range(parts):
        left = [0, 1, 2, 3]
        for axis in scatter_order(part):
            left.remove(axis)
            shape = (sizes[axis] - 1,) + tuple(sizes[a] for a in left) + grads[part].shape[4:]
            scratch.append(pltpu.VMEM(shape, jnp.bfloat16))
    for part in range(parts):
        left = [0, 1, 2, 3]
        for axis in scatter_order(part)[:3]:
            left.remove(axis)
            shape = tuple(sizes[a] for a in left) + grads[part].shape[4:]
            scratch.append(pltpu.VMEM(shape, jnp.bfloat16))
    outs = [jax.ShapeDtypeStruct(g.shape[4:], jnp.float32) for g in grads]
    args = list(grads)
    if gains is not None:
        args.append(gains)
        outs.append(jax.ShapeDtypeStruct(gains.shape, jnp.float32))
        scratch += [
            pltpu.VMEM((4, most - 1) + gains.shape, jnp.float32),
            pltpu.VMEM((4,) + gains.shape, jnp.float32),
            pltpu.SemaphoreType.DMA((4, most)),
            pltpu.SemaphoreType.DMA((4, most)),
        ]
    scratch += [pltpu.SemaphoreType.DMA((parts, 4, most))] * 2
    return pl.pallas_call(
        functools.partial(scatter_kernel, sizes, parts, int(gains is not None)),
        out_shape=outs,
        in_specs=[pl.BlockSpec(memory_space=pltpu.VMEM)] * len(args),
        out_specs=[pl.BlockSpec(memory_space=pltpu.VMEM)] * len(outs),
        scratch_shapes=scratch,
        compiler_params=pltpu.CompilerParams(
            collective_id=ident, has_side_effects=True, vmem_limit_bytes=VMEM_LIMIT
        ),
        cost_estimate=pl.CostEstimate(flops=0, bytes_accessed=60_000_000, transcendentals=0),
    )(*args)


def padded_rows(count):
    return -(-count // 2048) * 16


def pack(pieces, lead):
    flat = jnp.concatenate(pieces, axis=-1) if len(pieces) > 1 else pieces[0]
    rows = padded_rows(flat.shape[-1])
    flat = jnp.pad(flat, [(0, 0)] * len(lead) + [(0, rows * 128 - flat.shape[-1])])
    return flat.reshape(lead + (rows, 128))


def forward_kernel(tiles, bounds, q_ref, k_ref, vt_ref, index_ref, start_ref, o_ref, lse_ref):
    for tile in range(tiles):
        q = q_ref[0, tile]
        index, start = index_ref[tile], start_ref[tile]

        def step(block, carry, q=q, index=index, start=start):
            highest, acc = carry
            first = pl.multiple_of(block * BLK, BLK)
            k = k_ref[0, pl.ds(first, BLK), :]
            vt = vt_ref[0, :, pl.ds(first, BLK)]
            s = lax.dot_general(k, q, (((1,), (1,)), ((), ())), preferred_element_type=jnp.float32)
            row = first + lax.broadcasted_iota(jnp.int32, s.shape, 0)
            s = jnp.where((row <= index) & (row >= start), s, MASKED)
            new = jnp.maximum(highest, jnp.max(s, axis=0, keepdims=True))
            p = jnp.exp(s - new).astype(jnp.bfloat16)
            acc = acc * jnp.exp(highest - new) + jnp.dot(vt, p, preferred_element_type=jnp.float32)
            return new, acc

        width = q.shape[0]
        highest, acc = lax.fori_loop(
            bounds[tile, 0],
            bounds[tile, 1],
            step,
            (
                jnp.full((1, width), MASKED, jnp.float32),
                jnp.zeros((vt_ref.shape[1], width), jnp.float32),
            ),
        )
        total = acc[HEAD_SIZE : HEAD_SIZE + 1]
        o_ref[0, tile] = acc[:HEAD_SIZE] / total
        lse_ref[0, tile] = highest + jnp.log(total)


def backward_kernel(
    tiles, bounds, q_ref, do_ref, k_ref, kt_ref, v_ref, index_ref, start_ref, lse_ref, delta_ref,
    dq_ref, dk_ref, dv_ref, dk_acc, dv_acc,
):
    dk_acc[...] = jnp.zeros_like(dk_acc)
    dv_acc[...] = jnp.zeros_like(dv_acc)
    for tile in range(tiles):
        q, do = q_ref[0, tile], do_ref[0, tile]
        index, start = index_ref[tile], start_ref[tile]
        lse, delta = lse_ref[0, tile], delta_ref[0, tile]

        def step(block, dq, q=q, do=do, index=index, start=start, lse=lse, delta=delta):
            first = pl.multiple_of(block * BLK, BLK)
            rows = pl.ds(first, BLK)
            nt = (((1,), (1,)), ((), ()))
            s = lax.dot_general(k_ref[0, rows, :], q, nt, preferred_element_type=jnp.float32)
            dp = lax.dot_general(v_ref[0, rows, :], do, nt, preferred_element_type=jnp.float32)
            row = first + lax.broadcasted_iota(jnp.int32, s.shape, 0)
            s = jnp.where((row <= index) & (row >= start), s - lse, MASKED)
            p = jnp.exp(s)
            ds = (p * (dp - delta)).astype(jnp.bfloat16)
            dv_acc[rows, :] += jnp.dot(p.astype(jnp.bfloat16), do, preferred_element_type=jnp.float32)
            dk_acc[rows, :] += jnp.dot(ds, q, preferred_element_type=jnp.float32)
            return dq + jnp.dot(kt_ref[0, :, rows], ds, preferred_element_type=jnp.float32)

        dq_ref[0, tile] = lax.fori_loop(
            bounds[tile, 0],
            bounds[tile, 1],
            step,
            jnp.zeros((HEAD_SIZE, q.shape[0]), jnp.float32),
        )
    dk_ref[0] = dk_acc[...].astype(dk_ref.dtype)
    dv_ref[0] = dv_acc[...].astype(dv_ref.dtype)


def per_head(shape):
    return pl.BlockSpec((1,) + shape[1:], lambda g, b: (g,) + (0,) * (len(shape) - 1))


def for_all(shape):
    return pl.BlockSpec(shape, lambda g, b: (0,) * len(shape))


def attention_call(kernel, bounds, arrays, shared, out_shapes, scratch, flops):
    specs = [for_all(a.shape) if i in shared else per_head(a.shape) for i, a in enumerate(arrays)]
    return pl.pallas_call(
        functools.partial(kernel, bounds.shape[0]),
        out_shape=out_shapes,
        grid_spec=pltpu.PrefetchScalarGridSpec(
            num_scalar_prefetch=1,
            grid=(KEY_VALUE_HEADS,),
            in_specs=specs,
            out_specs=[per_head(o.shape) for o in out_shapes],
            scratch_shapes=scratch,
        ),
        compiler_params=pltpu.CompilerParams(vmem_limit_bytes=VMEM_LIMIT),
        cost_estimate=pl.CostEstimate(flops=flops, bytes_accessed=8_000_000, transcendentals=0),
    )(bounds, *arrays)


def per_device(sizes, layer_input, w_qkv, w_out, w_gu, w_down, norm_gains, lengths, cotangent):
    token_rows = layer_input.shape[0]
    seq_count = lax.axis_size("seq")
    group = token_rows * seq_count
    query_width = QUERY_HEADS * HEAD_SIZE
    key_width = KEY_VALUE_HEADS * HEAD_SIZE
    scale = 1.0 / math.sqrt(HEAD_SIZE)
    tiles = token_rows // BLK
    kvh = KEY_VALUE_HEADS
    count = math.prod(sizes)

    (qkv_all,) = all_gather([pack([w_qkv], ())], sizes, 0)
    mixing_in = qkv_all.reshape(count, -1)[:, : w_qkv.shape[0]].reshape(D, -1)

    query_index = lax.axis_index("seq") * token_rows + jnp.arange(token_rows, dtype=jnp.int32)
    start = layout(lengths[0], query_index)
    half = HEAD_SIZE // 2
    freq = jnp.exp(jnp.arange(half, dtype=jnp.float32) * (-2.0 * math.log(THETA) / HEAD_SIZE))
    angle = (query_index - start).astype(jnp.float32)[:, None] * freq[None, :]
    cosine, sine = jnp.cos(angle)[:, None, :], jnp.sin(angle)[:, None, :]

    def rotated(rows, sign):
        first, second = rows[..., :half], rows[..., half:]
        turn = sign * sine
        return jnp.concatenate(
            [first * cosine - second * turn, second * cosine + first * turn], axis=-1
        )

    inputs = layer_input.astype(jnp.float32)
    normed, norm_back = jax.vjp(rms_norm, inputs, norm_gains[0])
    normed_low = normed.astype(jnp.bfloat16)
    projected = jnp.dot(normed_low, mixing_in, preferred_element_type=jnp.float32)
    heads = projected[:, : query_width + key_width].reshape(token_rows, -1, HEAD_SIZE)
    turned = rotated(heads, 1.0).astype(jnp.bfloat16)
    pairs_mine = jnp.concatenate(
        [
            turned[:, QUERY_HEADS:].reshape(token_rows, key_width),
            projected[:, query_width + key_width :].astype(jnp.bfloat16),
        ],
        axis=1,
    )
    pairs = lax.all_gather(pairs_mine, "seq", axis=0, tiled=True)
    gu_all, rest_all = all_gather([pack([w_gu], ()), pack([w_out, w_down], ())], sizes, 1)
    expand_matrix = gu_all.reshape(count, -1)[:, : w_gu.shape[0]].reshape(D, 2 * FF)
    rest_flat = rest_all.reshape(count, -1)
    mixing_out = rest_flat[:, : w_out.shape[0]].reshape(query_width, D)
    shrink_matrix = rest_flat[:, w_out.shape[0] : w_out.shape[0] + w_down.shape[0]].reshape(FF, D)

    def stacked(rows):
        return (
            rows.reshape(tiles, BLK, kvh, HG, HEAD_SIZE)
            .transpose(2, 0, 3, 1, 4)
            .reshape(kvh, tiles, HG * BLK, HEAD_SIZE)
        )

    def unstacked(columns):
        return (
            columns.reshape(kvh, tiles, HEAD_SIZE, HG, BLK)
            .transpose(1, 4, 0, 3, 2)
            .reshape(token_rows, QUERY_HEADS, HEAD_SIZE)
        )

    def row_vector(values):
        return jnp.tile(values.reshape(tiles, 1, BLK), (1, 1, HG))

    query = stacked(turned[:, :QUERY_HEADS] * jnp.bfloat16(scale))
    kv = pairs.reshape(group, 2 * kvh, HEAD_SIZE).transpose(1, 0, 2)
    keys, values = kv[:kvh], kv[kvh:]
    kv_t = pairs.T.reshape(2 * kvh, HEAD_SIZE, group)
    keys_t = kv_t[:kvh]
    values_t = jnp.concatenate([kv_t[kvh:], jnp.ones((kvh, 16, group), jnp.bfloat16)], axis=1)
    index_rows, start_rows = row_vector(query_index), row_vector(start)
    bounds = jnp.stack([start[::BLK] // BLK, query_index[::BLK] // BLK + 1], axis=1)

    width = HG * BLK
    f32 = jnp.float32
    column_shape = jax.ShapeDtypeStruct((kvh, tiles, HEAD_SIZE, width), f32)
    attended_t, lse = attention_call(
        forward_kernel,
        bounds,
        [query, keys, values_t, index_rows, start_rows],
        (3, 4),
        [column_shape, jax.ShapeDtypeStruct((kvh, tiles, 1, width), f32)],
        [],
        10_000_000_000,
    )
    attended_rows = unstacked(attended_t)
    attended_low = attended_rows.reshape(token_rows, query_width).astype(jnp.bfloat16)
    mid = inputs + jnp.dot(attended_low, mixing_out, preferred_element_type=f32)
    normed_two, norm_two_back = jax.vjp(rms_norm, mid, norm_gains[1])
    normed_two_low = normed_two.astype(jnp.bfloat16)
    gate_up = jnp.dot(normed_two_low, expand_matrix, preferred_element_type=f32)
    hidden, hidden_back = jax.vjp(silu_product, gate_up)
    hidden_low = hidden.astype(jnp.bfloat16)
    result = (mid + jnp.dot(hidden_low, shrink_matrix, preferred_element_type=f32)).astype(
        jnp.bfloat16
    )
    grad_down = jnp.einsum("tf,td->fd", hidden_low, cotangent, preferred_element_type=f32)
    d_hidden = jnp.einsum("td,fd->tf", cotangent, shrink_matrix, preferred_element_type=f32)
    d_gate_up = hidden_back(d_hidden)[0].astype(jnp.bfloat16)
    grad_expand = jnp.einsum("td,tf->df", normed_two_low, d_gate_up, preferred_element_type=f32)
    d_normed_two = jnp.einsum("tf,df->td", d_gate_up, expand_matrix, preferred_element_type=f32)
    d_mid_part, grad_gain_two = norm_two_back(d_normed_two)
    d_mid = cotangent.astype(f32) + d_mid_part
    d_branch = d_mid.astype(jnp.bfloat16)
    grad_mixing_out = jnp.einsum("tq,td->qd", attended_low, d_branch, preferred_element_type=f32)
    d_attended = jnp.einsum("td,qd->tq", d_branch, mixing_out, preferred_element_type=f32).astype(
        jnp.bfloat16
    )
    delta = jnp.sum(
        d_attended.reshape(token_rows, QUERY_HEADS, HEAD_SIZE).astype(f32) * attended_rows, axis=-1
    )
    delta_rows = (
        delta.reshape(tiles, BLK, kvh, HG).transpose(2, 0, 3, 1).reshape(kvh, tiles, 1, width)
    )
    pair_shape = jax.ShapeDtypeStruct((kvh, group, HEAD_SIZE), jnp.bfloat16)
    d_query_t, d_keys, d_values = attention_call(
        backward_kernel,
        bounds,
        [query, stacked(d_attended), keys, keys_t, values, index_rows, start_rows, lse, delta_rows],
        (5, 6),
        [column_shape, pair_shape, pair_shape],
        [pltpu.VMEM((group, HEAD_SIZE), f32)] * 2,
        25_000_000_000,
    )
    d_pairs = jnp.concatenate([d_keys, d_values], axis=0).transpose(1, 0, 2)
    d_pairs_mine = lax.psum_scatter(
        d_pairs.reshape(group, 2 * key_width), "seq", scatter_dimension=0, tiled=True
    ).astype(f32)

    def by_owner(grad):
        return grad.astype(jnp.bfloat16).reshape(sizes + (-1,))

    gu_mine, rest_mine = reduce_scatter(
        [pack([by_owner(grad_expand)], sizes), pack([by_owner(grad_mixing_out), by_owner(grad_down)], sizes)],
        None,
        sizes,
        2,
    )
    d_query = unstacked(d_query_t) * scale
    d_turned = jnp.concatenate(
        [d_query, d_pairs_mine[:, :key_width].reshape(token_rows, kvh, HEAD_SIZE)], axis=1
    )
    d_projected = jnp.concatenate(
        [rotated(d_turned, -1.0).reshape(token_rows, -1), d_pairs_mine[:, key_width:]], axis=1
    ).astype(jnp.bfloat16)
    grad_mixing_in = jnp.einsum("td,tq->dq", normed_low, d_projected, preferred_element_type=f32)
    d_normed = jnp.einsum("tq,dq->td", d_projected, mixing_in, preferred_element_type=f32)
    d_input_part, grad_gain_one = norm_back(d_normed)
    gains = jnp.stack([grad_gain_one, grad_gain_two])
    qkv_mine, gains_sum = reduce_scatter(
        [pack([by_owner(grad_mixing_in)], sizes)], gains, sizes, 3
    )
    rest_row = rest_mine.reshape(-1)
    cut = w_out.shape[0]
    return (
        result,
        d_mid + d_input_part,
        qkv_mine.reshape(-1)[: w_qkv.shape[0]],
        rest_row[:cut],
        gu_mine.reshape(-1)[: w_gu.shape[0]],
        rest_row[cut : cut + w_down.shape[0]],
        gains_sum,
    )


def solution(mesh):
    spread = P(("seq", "dp"))
    rows = P(("seq", "dp"), None)
    return jax.shard_map(
        functools.partial(per_device, grid_sizes(mesh.shape["seq"], mesh.shape["dp"])),
        mesh=mesh,
        in_specs=(rows, spread, spread, spread, spread, P(), P("dp", None), rows),
        out_specs=(rows, rows, spread, spread, spread, spread, P()),
        check_vma=False,
    )
```

```python
import functools
import math

import jax
import jax.numpy as jnp
from jax import lax
from jax.experimental import pallas as pl
from jax.experimental.pallas import tpu as pltpu
from jax.sharding import PartitionSpec as P

D = 576
QUERY_HEADS = 9
KEY_VALUE_HEADS = 3
HEAD_SIZE = 64
FF = 1536
HG = QUERY_HEADS // KEY_VALUE_HEADS

EPS = 1e-05
THETA = 100000.0
MASKED = -1e30
MESH = pl.DeviceIdType.MESH
BLK = 256
VMEM_LIMIT = 56 * 1024 * 1024
ORDERS = ((0, 2, 1), (1, 0, 2), (1, 0, 2))


def rms_norm(value_rows, gain):
    return (
        value_rows
        * lax.rsqrt(jnp.mean(value_rows * value_rows, axis=-1, keepdims=True) + EPS)
        * gain
    )


def layout(lengths_row, index):
    count = lengths_row.shape[0]
    earlier = jnp.arange(count)[:, None] >= jnp.arange(count)[None, :]
    ends = jnp.sum(jnp.where(earlier, lengths_row[None, :], 0), axis=1, dtype=jnp.int32)
    done = ends[None, :] <= index[:, None]
    return jnp.sum(jnp.where(done, lengths_row[None, :], 0), axis=1, dtype=jnp.int32)


def silu_product(gate_up):
    width = gate_up.shape[1] // 2
    return jax.nn.silu(gate_up[:, :width]) * gate_up[:, width:]


def grid_sizes(seq_count, dp_count):
    return (seq_count // 2, 2, dp_count // 2, 2)


def coords():
    seq, dp = lax.axis_index("seq"), lax.axis_index("dp")
    return [seq // 2, seq % 2, dp // 2, dp % 2]


def device_at(coord):
    return (coord[0] * 2 + coord[1], coord[2] * 2 + coord[3])


def moved(me, sizes, axis, step):
    other = list(me)
    other[axis] = lax.rem(me[axis] + step + sizes[axis], sizes[axis])
    return other


def greet(me, sizes):
    barrier = pltpu.get_barrier_semaphore()
    count = 0
    for axis in range(4):
        for step in range(1, sizes[axis]):
            pl.semaphore_signal(
                barrier,
                inc=1,
                device_id=device_at(moved(me, sizes, axis, step)),
                device_id_type=MESH,
            )
            count += 1
    pl.semaphore_wait(barrier, count)


def gather_kernel(sizes, parts, *refs):
    shards, outs = refs[:parts], refs[parts : 2 * parts]
    send, recv, core_send, core_recv, local = refs[2 * parts :]
    me = coords()
    greet(me, sizes)
    started = []
    for part in range(parts):
        own = pltpu.make_async_copy(
            shards[part], outs[part].at[me[0], me[1], me[2], me[3]], local.at[part]
        )
        own.start()
        started.append(own)
    for own in started:
        own.wait()

    def region(part, held, where):
        return outs[part].at[
            tuple(slice(None) if a in held else where[a] for a in range(3)) + (where[3],)
        ]

    def copy(part, phase, axis, held, step, arriving=False):
        where = moved(me, sizes, axis, -step) if arriving else me
        block = region(part, held, where)
        return pltpu.make_async_remote_copy(
            src_ref=block,
            dst_ref=block,
            send_sem=send.at[part, phase, step],
            recv_sem=recv.at[part, phase, step],
            device_id=device_at(moved(me, sizes, axis, step)),
            device_id_type=MESH,
        )

    def to_core(part, slot, held, where, arriving=False):
        there = moved(where, sizes, 3, 1) if arriving else where
        block = region(part, held, there)
        return pltpu.make_async_remote_copy(
            src_ref=block,
            dst_ref=block,
            send_sem=core_send.at[part, slot],
            recv_sem=core_recv.at[part, slot],
            device_id=device_at(moved(me, sizes, 3, 1)),
            device_id_type=MESH,
        )

    for part in range(parts):
        axis = ORDERS[part][0]
        for step in range(1, sizes[axis]):
            copy(part, 0, axis, (), step).start()
    pending = []
    for phase in range(3):
        for part in range(parts):
            axis = ORDERS[part][phase]
            held = ORDERS[part][:phase]
            for step in range(1, sizes[axis]):
                copy(part, phase, axis, held, step, arriving=True).wait_recv()
                if phase == 2:
                    origin = moved(me, sizes, axis, -step)
                    to_core(part, step, held, origin).start()
                    pending.append((part, step, held, origin))
            if phase < 2:
                following = ORDERS[part][phase + 1]
                for step in range(1, sizes[following]):
                    copy(part, phase + 1, following, ORDERS[part][: phase + 1], step).start()
            if phase == 1:
                to_core(part, 0, ORDERS[part][:2], me).start()
                pending.append((part, 0, ORDERS[part][:2], me))
    for part in range(parts):
        for phase in range(3):
            axis = ORDERS[part][phase]
            for step in range(1, sizes[axis]):
                copy(part, phase, axis, ORDERS[part][:phase], step).wait_send()
    for part, slot, held, origin in pending:
        to_core(part, slot, held, origin).wait_send()
        to_core(part, slot, held, origin, arriving=True).wait_recv()


def all_gather(shards, sizes, ident):
    parts = len(shards)
    most = max(sizes)
    return pl.pallas_call(
        functools.partial(gather_kernel, sizes, parts),
        out_shape=[jax.ShapeDtypeStruct(sizes + s.shape, s.dtype) for s in shards],
        in_specs=[pl.BlockSpec(memory_space=pltpu.VMEM)] * parts,
        out_specs=[pl.BlockSpec(memory_space=pltpu.VMEM)] * parts,
        scratch_shapes=[
            pltpu.SemaphoreType.DMA((parts, 3, most)),
            pltpu.SemaphoreType.DMA((parts, 3, most)),
            pltpu.SemaphoreType.DMA((parts, most)),
            pltpu.SemaphoreType.DMA((parts, most)),
            pltpu.SemaphoreType.DMA((parts,)),
        ],
        compiler_params=pltpu.CompilerParams(
            collective_id=ident, has_side_effects=True, vmem_limit_bytes=VMEM_LIMIT
        ),
        cost_estimate=pl.CostEstimate(flops=0, bytes_accessed=60_000_000, transcendentals=0),
    )(*shards)


def scatter_order(part):
    return (3,) + tuple(reversed(ORDERS[part]))


def scatter_kernel(sizes, parts, with_gains, *refs):
    n_in = parts + with_gains
    grads, outs = refs[:n_in], refs[n_in : 2 * n_in]
    rest = list(refs[2 * n_in :])
    arrived = [[rest.pop(0) for _ in range(4)] for _ in range(parts)]
    totals = [[rest.pop(0) for _ in range(3)] for _ in range(parts)]
    if with_gains:
        gain_arrived, gain_total = rest.pop(0), rest.pop(0)
        gain_send, gain_recv = rest.pop(0), rest.pop(0)
    send, recv = rest
    me = coords()
    greet(me, sizes)

    def held_ref(part, phase):
        return grads[part] if phase == 0 else totals[part][phase - 1]

    def view(part, phase, index):
        order = scatter_order(part)
        left = sorted(set(range(4)) - set(order[:phase]))
        return tuple(index if a == order[phase] else slice(None) for a in left)

    def copy(part, phase, step):
        axis = scatter_order(part)[phase]
        target = moved(me, sizes, axis, step)
        return pltpu.make_async_remote_copy(
            src_ref=held_ref(part, phase).at[view(part, phase, target[axis])],
            dst_ref=arrived[part][phase].at[step - 1],
            send_sem=send.at[part, phase, step],
            recv_sem=recv.at[part, phase, step],
            device_id=device_at(target),
            device_id_type=MESH,
        )

    def add(part, phase):
        axis = scatter_order(part)[phase]
        mine = held_ref(part, phase).at[view(part, phase, me[axis])]
        lead = mine.shape[:-2]
        others = arrived[part][phase]

        def total_at(place):
            value = mine[place].astype(jnp.float32)
            for step in range(1, sizes[axis]):
                value = value + others[(step - 1,) + place].astype(jnp.float32)
            return value

        if phase == 3:
            outs[part][...] = total_at((slice(None), slice(None)))
            return
        target = totals[part][phase]

        def body(flat, carry):
            place = []
            for size in reversed(lead):
                place.insert(0, lax.rem(flat, size))
                flat = flat // size
            place = tuple(place) + (slice(None), slice(None))
            target[place] = total_at(place).astype(target.dtype)
            return carry

        lax.fori_loop(0, math.prod(lead), body, 0)

    def gain_copy(phase, step):
        return pltpu.make_async_remote_copy(
            src_ref=gain_total.at[phase],
            dst_ref=gain_arrived.at[phase, step - 1],
            send_sem=gain_send.at[phase, step],
            recv_sem=gain_recv.at[phase, step],
            device_id=device_at(moved(me, sizes, phase, step)),
            device_id_type=MESH,
        )

    def start(phase, part):
        for step in range(1, sizes[scatter_order(part)[phase]]):
            copy(part, phase, step).start()

    def gain_start(phase):
        for step in range(1, sizes[phase]):
            gain_copy(phase, step).start()

    for part in range(parts):
        start(0, part)
    if with_gains:
        gain_total[0] = grads[parts][...]
        gain_start(0)
    for phase in range(4):
        for part in reversed(range(parts)):
            for step in range(1, sizes[scatter_order(part)[phase]]):
                copy(part, phase, step).wait_recv()
            add(part, phase)
            if phase < 3:
                start(phase + 1, part)
        if with_gains:
            value = gain_total[phase]
            for step in range(1, sizes[phase]):
                gain_copy(phase, step).wait_recv()
            slots = [value] + [gain_arrived[phase, s - 1] for s in range(1, sizes[phase])]
            value = sum(slots[1:], slots[0])
            if phase < 3:
                gain_total[phase + 1] = value
                gain_start(phase + 1)
            else:
                outs[parts][...] = value
    for phase in range(4):
        for part in range(parts):
            for step in range(1, sizes[scatter_order(part)[phase]]):
                copy(part, phase, step).wait_send()
        if with_gains:
            for step in range(1, sizes[phase]):
                gain_copy(phase, step).wait_send()


def reduce_scatter(grads, gains, sizes, ident):
    parts = len(grads)
    most = max(sizes)
    scratch = []
    for part in range(parts):
        left = [0, 1, 2, 3]
        for axis in scatter_order(part):
            left.remove(axis)
            shape = (sizes[axis] - 1,) + tuple(sizes[a] for a in left) + grads[part].shape[4:]
            scratch.append(pltpu.VMEM(shape, jnp.bfloat16))
    for part in range(parts):
        left = [0, 1, 2, 3]
        for axis in scatter_order(part)[:3]:
            left.remove(axis)
            shape = tuple(sizes[a] for a in left) + grads[part].shape[4:]
            scratch.append(pltpu.VMEM(shape, jnp.bfloat16))
    outs = [jax.ShapeDtypeStruct(g.shape[4:], jnp.float32) for g in grads]
    args = list(grads)
    if gains is not None:
        args.append(gains)
        outs.append(jax.ShapeDtypeStruct(gains.shape, jnp.float32))
        scratch += [
            pltpu.VMEM((4, most - 1) + gains.shape, jnp.float32),
            pltpu.VMEM((4,) + gains.shape, jnp.float32),
            pltpu.SemaphoreType.DMA((4, most)),
            pltpu.SemaphoreType.DMA((4, most)),
        ]
    scratch += [pltpu.SemaphoreType.DMA((parts, 4, most))] * 2
    return pl.pallas_call(
        functools.partial(scatter_kernel, sizes, parts, int(gains is not None)),
        out_shape=outs,
        in_specs=[pl.BlockSpec(memory_space=pltpu.VMEM)] * len(args),
        out_specs=[pl.BlockSpec(memory_space=pltpu.VMEM)] * len(outs),
        scratch_shapes=scratch,
        compiler_params=pltpu.CompilerParams(
            collective_id=ident, has_side_effects=True, vmem_limit_bytes=VMEM_LIMIT
        ),
        cost_estimate=pl.CostEstimate(flops=0, bytes_accessed=60_000_000, transcendentals=0),
    )(*args)


def padded_rows(count):
    return -(-count // 2048) * 16


def pack(flat, lead):
    size = flat.shape[-1]
    rows = padded_rows(size)
    none = [(0, 0)] * len(lead)
    if size % 128 == 0:
        flat = flat.reshape(lead + (size // 128, 128))
        return jnp.pad(flat, none + [(0, rows - size // 128), (0, 0)])
    return jnp.pad(flat, none + [(0, rows * 128 - size)]).reshape(lead + (rows, 128))


def unpack(packed, lead, size):
    if size % 128 == 0:
        return packed[..., : size // 128, :].reshape(lead + (size,))
    return packed.reshape(lead + (-1,))[..., :size]


def dot_rows(left, right):
    return lax.dot_general(left, right, (((1,), (1,)), ((), ())), preferred_element_type=jnp.float32)


def dot_columns(left, right):
    return lax.dot_general(left, right, (((0,), (0,)), ((), ())), preferred_element_type=jnp.float32)


def head_columns(head):
    first = head * HEAD_SIZE
    second = first + KEY_VALUE_HEADS * HEAD_SIZE
    return slice(first, first + HEAD_SIZE), slice(second, second + HEAD_SIZE)


def forward_kernel(tiles, bounds, q_ref, kv_ref, index_ref, start_ref, o_ref, lse_ref):
    for tile, head in [(t, h) for t in range(tiles) for h in range(KEY_VALUE_HEADS)]:
        key_part, value_part = head_columns(head)
        q = q_ref[head, tile]
        index, start = index_ref[tile], start_ref[tile]

        def step(block, carry, q=q, index=index, start=start, cut=(key_part, value_part)):
            highest, total, acc = carry
            first = pl.multiple_of(block * BLK, BLK)
            rows = pl.ds(first, BLK)
            s = dot_rows(kv_ref[rows, cut[0]], q)
            row = first + lax.broadcasted_iota(jnp.int32, s.shape, 0)
            s = jnp.where((row <= index) & (row >= start), s, MASKED)
            new = jnp.maximum(highest, jnp.max(s, axis=0, keepdims=True))
            p = jnp.exp(s - new)
            fade = jnp.exp(highest - new)
            total = total * fade + jnp.sum(p, axis=0, keepdims=True)
            acc = acc * fade + dot_columns(kv_ref[rows, cut[1]], p.astype(jnp.bfloat16))
            return new, total, acc

        width = q.shape[0]
        highest, total, acc = lax.fori_loop(
            bounds[tile, 0],
            bounds[tile, 1],
            step,
            (
                jnp.full((1, width), MASKED, jnp.float32),
                jnp.zeros((1, width), jnp.float32),
                jnp.zeros((HEAD_SIZE, width), jnp.float32),
            ),
        )
        o_ref[head, tile] = acc / total
        lse_ref[head, tile] = highest + jnp.log(total)


def backward_kernel(
    tiles, bounds, q_ref, do_ref, kv_ref, index_ref, start_ref, lse_ref, delta_ref,
    dq_ref, dkv_ref, *accs,
):
    for acc in accs:
        acc[...] = jnp.zeros_like(acc)
    for tile, head in [(t, h) for t in range(tiles) for h in range(KEY_VALUE_HEADS)]:
        q, do = q_ref[head, tile], do_ref[head, tile]
        index, start = index_ref[tile], start_ref[tile]
        lse, delta = lse_ref[head, tile], delta_ref[head, tile]

        def step(block, dq, head=head, q=q, do=do, index=index, start=start, lse=lse, delta=delta):
            key_part, value_part = head_columns(head)
            dk_acc, dv_acc = accs[head], accs[KEY_VALUE_HEADS + head]
            first = pl.multiple_of(block * BLK, BLK)
            rows = pl.ds(first, BLK)
            k = kv_ref[rows, key_part]
            s = dot_rows(k, q)
            dp = dot_rows(kv_ref[rows, value_part], do)
            row = first + lax.broadcasted_iota(jnp.int32, s.shape, 0)
            s = jnp.where((row <= index) & (row >= start), s - lse, MASKED)
            p = jnp.exp(s)
            ds = (p * (dp - delta)).astype(jnp.bfloat16)
            dv_acc[rows, :] += jnp.dot(p.astype(jnp.bfloat16), do, preferred_element_type=jnp.float32)
            dk_acc[rows, :] += jnp.dot(ds, q, preferred_element_type=jnp.float32)
            return dq + dot_columns(k, ds)

        dq_ref[head, tile] = lax.fori_loop(
            bounds[tile, 0],
            bounds[tile, 1],
            step,
            jnp.zeros((HEAD_SIZE, q.shape[0]), jnp.float32),
        )

    def write(block, carry):
        rows = pl.ds(pl.multiple_of(block * BLK, BLK), BLK)
        dkv_ref[rows, :] = jnp.concatenate([acc[rows, :] for acc in accs], axis=1).astype(
            dkv_ref.dtype
        )
        return carry

    lax.fori_loop(0, dkv_ref.shape[0] // BLK, write, 0)


def attention_call(kernel, bounds, arrays, out_shapes, scratch, flops):
    whole = pl.BlockSpec(memory_space=pltpu.VMEM)
    return pl.pallas_call(
        functools.partial(kernel, bounds.shape[0]),
        out_shape=out_shapes,
        in_specs=[pl.BlockSpec(memory_space=pltpu.SMEM)] + [whole] * len(arrays),
        out_specs=[whole] * len(out_shapes),
        scratch_shapes=scratch,
        compiler_params=pltpu.CompilerParams(vmem_limit_bytes=VMEM_LIMIT),
        cost_estimate=pl.CostEstimate(flops=flops, bytes_accessed=8_000_000, transcendentals=0),
    )(bounds, *arrays)


def per_device(sizes, layer_input, w_qkv, w_out, w_gu, w_down, norm_gains, lengths, cotangent):
    token_rows = layer_input.shape[0]
    seq_count = lax.axis_size("seq")
    group = token_rows * seq_count
    query_width = QUERY_HEADS * HEAD_SIZE
    key_width = KEY_VALUE_HEADS * HEAD_SIZE
    scale = 1.0 / math.sqrt(HEAD_SIZE)
    tiles = token_rows // BLK
    kvh = KEY_VALUE_HEADS

    (qkv_all,) = all_gather([pack(w_qkv, ())], sizes, 0)
    mixing_in = unpack(qkv_all, sizes, w_qkv.shape[0]).reshape(D, -1)

    query_index = lax.axis_index("seq") * token_rows + jnp.arange(token_rows, dtype=jnp.int32)
    start = layout(lengths[0], query_index)
    half = HEAD_SIZE // 2
    freq = jnp.exp(jnp.arange(half, dtype=jnp.float32) * (-2.0 * math.log(THETA) / HEAD_SIZE))
    angle = (query_index - start).astype(jnp.float32)[:, None] * freq[None, :]
    cosine, sine = jnp.cos(angle)[:, None, :], jnp.sin(angle)[:, None, :]

    def rotated(rows, sign):
        first, second = rows[..., :half], rows[..., half:]
        turn = sign * sine
        return jnp.concatenate(
            [first * cosine - second * turn, second * cosine + first * turn], axis=-1
        )

    inputs = layer_input.astype(jnp.float32)
    normed, norm_back = jax.vjp(rms_norm, inputs, norm_gains[0])
    normed_low = normed.astype(jnp.bfloat16)
    projected = jnp.dot(normed_low, mixing_in, preferred_element_type=jnp.float32)
    heads = projected[:, : query_width + key_width].reshape(token_rows, -1, HEAD_SIZE)
    turned = rotated(heads, 1.0).astype(jnp.bfloat16)
    pairs_mine = jnp.concatenate(
        [
            turned[:, QUERY_HEADS:].reshape(token_rows, key_width),
            projected[:, query_width + key_width :].astype(jnp.bfloat16),
        ],
        axis=1,
    )
    pairs = lax.all_gather(pairs_mine, "seq", axis=0, tiled=True)
    gathered = all_gather([pack(w, ()) for w in (w_gu, w_down, w_out)], sizes, 1)
    expand_matrix = unpack(gathered[0], sizes, w_gu.shape[0]).reshape(D, 2 * FF)
    shrink_matrix = unpack(gathered[1], sizes, w_down.shape[0]).reshape(FF, D)
    mixing_out = unpack(gathered[2], sizes, w_out.shape[0]).reshape(query_width, D)

    def stacked(rows):
        return (
            rows.reshape(tiles, BLK, kvh, HG, HEAD_SIZE)
            .transpose(2, 0, 3, 1, 4)
            .reshape(kvh, tiles, HG * BLK, HEAD_SIZE)
        )

    def unstacked(columns):
        return (
            columns.reshape(kvh, tiles, HEAD_SIZE, HG, BLK)
            .transpose(1, 4, 0, 3, 2)
            .reshape(token_rows, QUERY_HEADS, HEAD_SIZE)
        )

    def row_vector(values):
        return jnp.tile(values.reshape(tiles, 1, BLK), (1, 1, HG))

    query = stacked(turned[:, :QUERY_HEADS] * jnp.bfloat16(scale))
    index_rows, start_rows = row_vector(query_index), row_vector(start)
    bounds = jnp.stack([start[::BLK] // BLK, query_index[::BLK] // BLK + 1], axis=1)

    width = HG * BLK
    f32 = jnp.float32
    column_shape = jax.ShapeDtypeStruct((kvh, tiles, HEAD_SIZE, width), f32)
    attended_t, lse = attention_call(
        forward_kernel,
        bounds,
        [query, pairs, index_rows, start_rows],
        [column_shape, jax.ShapeDtypeStruct((kvh, tiles, 1, width), f32)],
        [],
        10_000_000_000,
    )
    attended_rows = unstacked(attended_t)
    attended_low = attended_rows.reshape(token_rows, query_width).astype(jnp.bfloat16)
    mid = inputs + jnp.dot(attended_low, mixing_out, preferred_element_type=f32)
    normed_two, norm_two_back = jax.vjp(rms_norm, mid, norm_gains[1])
    normed_two_low = normed_two.astype(jnp.bfloat16)
    gate_up = jnp.dot(normed_two_low, expand_matrix, preferred_element_type=f32)
    hidden, hidden_back = jax.vjp(silu_product, gate_up)
    hidden_low = hidden.astype(jnp.bfloat16)
    result = (mid + jnp.dot(hidden_low, shrink_matrix, preferred_element_type=f32)).astype(
        jnp.bfloat16
    )
    grad_down = jnp.einsum("tf,td->fd", hidden_low, cotangent, preferred_element_type=f32)
    d_hidden = jnp.einsum("td,fd->tf", cotangent, shrink_matrix, preferred_element_type=f32)
    d_gate_up = hidden_back(d_hidden)[0].astype(jnp.bfloat16)
    grad_expand = jnp.einsum("td,tf->df", normed_two_low, d_gate_up, preferred_element_type=f32)
    d_normed_two = jnp.einsum("tf,df->td", d_gate_up, expand_matrix, preferred_element_type=f32)
    d_mid_part, grad_gain_two = norm_two_back(d_normed_two)
    d_mid = cotangent.astype(f32) + d_mid_part
    d_branch = d_mid.astype(jnp.bfloat16)
    grad_mixing_out = jnp.einsum("tq,td->qd", attended_low, d_branch, preferred_element_type=f32)
    d_attended = jnp.einsum("td,qd->tq", d_branch, mixing_out, preferred_element_type=f32).astype(
        jnp.bfloat16
    )
    delta = jnp.sum(
        d_attended.reshape(token_rows, QUERY_HEADS, HEAD_SIZE).astype(f32) * attended_rows, axis=-1
    )
    delta_rows = (
        delta.reshape(tiles, BLK, kvh, HG).transpose(2, 0, 3, 1).reshape(kvh, tiles, 1, width)
    )
    d_query_t, d_pairs = attention_call(
        backward_kernel,
        bounds,
        [query, stacked(d_attended), pairs, index_rows, start_rows, lse, delta_rows],
        [column_shape, jax.ShapeDtypeStruct(pairs.shape, jnp.bfloat16)],
        [pltpu.VMEM((group, HEAD_SIZE), f32)] * (2 * kvh),
        25_000_000_000,
    )
    d_pairs_mine = lax.psum_scatter(
        d_pairs, "seq", scatter_dimension=0, tiled=True
    ).astype(f32)

    def by_owner(grad):
        return grad.astype(jnp.bfloat16).reshape(sizes + (-1,))

    gu_mine, down_mine, out_mine = reduce_scatter(
        [pack(by_owner(g), sizes) for g in (grad_expand, grad_down, grad_mixing_out)],
        None,
        sizes,
        2,
    )
    d_query = unstacked(d_query_t) * scale
    d_turned = jnp.concatenate(
        [d_query, d_pairs_mine[:, :key_width].reshape(token_rows, kvh, HEAD_SIZE)], axis=1
    )
    d_projected = jnp.concatenate(
        [rotated(d_turned, -1.0).reshape(token_rows, -1), d_pairs_mine[:, key_width:]], axis=1
    ).astype(jnp.bfloat16)
    grad_mixing_in = jnp.einsum("td,tq->dq", normed_low, d_projected, preferred_element_type=f32)
    d_normed = jnp.einsum("tq,dq->td", d_projected, mixing_in, preferred_element_type=f32)
    d_input_part, grad_gain_one = norm_back(d_normed)
    gains = jnp.stack([grad_gain_one, grad_gain_two])
    qkv_mine, gains_sum = reduce_scatter(
        [pack(by_owner(grad_mixing_in), sizes)], gains, sizes, 3
    )
    return (
        result,
        d_mid + d_input_part,
        unpack(qkv_mine, (), w_qkv.shape[0]),
        unpack(out_mine, (), w_out.shape[0]),
        unpack(gu_mine, (), w_gu.shape[0]),
        unpack(down_mine, (), w_down.shape[0]),
        gains_sum,
    )


def solution(mesh):
    spread = P(("seq", "dp"))
    rows = P(("seq", "dp"), None)
    return jax.shard_map(
        functools.partial(per_device, grid_sizes(mesh.shape["seq"], mesh.shape["dp"])),
        mesh=mesh,
        in_specs=(rows, spread, spread, spread, spread, P(), P("dp", None), rows),
        out_specs=(rows, rows, spread, spread, spread, spread, P()),
        check_vma=False,
    )
```
